32 devices in a mesh: gx: 8 (over y, x, core), gy: 4 (over z).
Axes of the slice: x: 2, y: 2, z: 4, core: 2. Of those that a mesh axis runs over, the one named last changes fastest.
Arguments:
- u_flow: bfloat16 [16, 1152, 512], P(None, 'gx', 'gy'), may hold values from -6 to 6
- v_flow: bfloat16 [16, 1152, 512], P(None, 'gx', 'gy'), may hold values from -6 to 6
- sea_mask: int32 [1152, 512], P('gx', 'gy'), may hold values 0 or 1
- bottom_level: int32 [1152, 512], P('gx', 'gy'), may hold values from 1 to 16
- mode_project: bfloat16 [16, 2], replicated, may hold values from -1.5 to 1.5
- mode_shape: float32 [16, 2], replicated, may hold values from -4 to 4
- forward_x: bfloat16 [1152, 1152], P('gx'), may hold values from -0.1875 to 0.1875
- forward_y: bfloat16 [512, 512], P('gy'), may hold values from -0.25 to 0.25
- inverse_x: bfloat16 [1152, 1152], P('gx'), may hold values from -0.1875 to 0.1875
- inverse_y: bfloat16 [512, 512], P('gy'), may hold values from -0.25 to 0.25
- eigen_x: float32 [1152], P('gx'), may hold values from 0.5 to 4
- eigen_y: float32 [512], P('gy'), may hold values from 0.5 to 4
- mode_shift: float32 [2], replicated, may hold values from 0.5 to 2
Outputs:
- u_correct: bfloat16 [16, 1152, 512], P(None, 'gx', 'gy')
- v_correct: bfloat16 [16, 1152, 512], P(None, 'gx', 'gy')
- pressure: float32 [2, 1152, 512], P(None, 'gx', 'gy')
The draws below stay inside these ranges and needn't reach their ends.
Inputs may be any that keep to these rules, and one draw needn't show every extreme that they name: `sea_mask`: land and sea flags.
All inputs are finite; a program needn't handle non-finite values. No bound on the sum of `sea_mask` on one device may be relied on, other than what follows from the above.
Results may differ from the reference program's by a relative error of at most 0.014.
Values may be sent and summed in bfloat16 or wider, within the bound.
A program may use at most 64 MiB of HBM per device.

```python
import math
import jax
import jax.numpy as jnp
from jax import lax

LEV = 16
MODES = 2
NX = 1152
NY = 512


def with_ends(result, key, least, top_value):
    longest = result.shape.index(max(result.shape))
    spots = []
    for shift in (0, 1):
        where = [jax.random.randint(jax.random.fold_in(key, axis), (), 0, length) for axis, length in enumerate(result.shape)]
        where[longest] = (where[longest] + shift) % result.shape[longest]
        spots.append(tuple(where))
    return result.at[spots[0]].set(least).at[spots[1]].set(top_value)


def steps_of(key, dims, shards, low, high):
    loudness, own = 1.0, jax.random.fold_in(key, 6)
    for axis_at, blocks in shards:
        heights = jnp.exp(jax.random.uniform(jax.random.fold_in(own, axis_at), (blocks,), jnp.float32, low / len(shards), high / len(shards)))
        loudness = loudness * jnp.repeat(heights, dims[axis_at] // blocks).reshape([-1 if axis == axis_at else 1 for axis in range(len(dims))])
    return loudness


def bell_draw(rng, dims, deviation, limit, shards=(), kind=jnp.bfloat16):
    drawn = jax.random.normal(rng, dims, jnp.float32) * deviation
    if len(shards) > 0:
        drawn = steps_of(rng, dims, shards, -0.22, 0.18) * drawn
    return jnp.clip(drawn, min=-limit, max=limit).astype(kind)


def setup_inputs(seed: int = 0) -> dict:
    keys = jax.random.split(jax.random.key(seed), 14)
    u_flow = bell_draw(keys[0], (LEV, NX, NY), 1.0, 6.0, ((1, 8), (2, 4)))
    v_flow = bell_draw(keys[1], (LEV, NX, NY), 1.0, 6.0, ((1, 8), (2, 4)))
    sea_mask = with_ends((jax.random.randint(keys[2], (NX, NY), 0, 4) < 3).astype(jnp.int32), jax.random.fold_in(keys[2], 1), 0, 1)
    bottom_level = with_ends(jax.random.randint(keys[3], (NX, NY), 1, LEV + 1), jax.random.fold_in(keys[3], 1), 1, LEV).astype(jnp.int32)
    mode_project = bell_draw(keys[4], (LEV, MODES), LEV ** -0.5, 1.5)
    mode_shape = bell_draw(keys[5], (LEV, MODES), 1.0, 4.0, (), jnp.float32)
    forward_x = bell_draw(keys[6], (NX, NX), NX ** -0.5, 0.1875, ((0, 8),))
    forward_y = bell_draw(keys[7], (NY, NY), NY ** -0.5, 0.25, ((0, 4),))
    inverse_x = bell_draw(keys[8], (NX, NX), NX ** -0.5, 0.1875, ((0, 8),))
    inverse_y = bell_draw(keys[9], (NY, NY), NY ** -0.5, 0.25, ((0, 4),))
    eigen_x = jnp.clip(jnp.exp(math.log(4.0) - 2.0794415 * jax.random.uniform(keys[10], (NX,), jnp.float32) ** steps_of(keys[10], (NX,), ((0, 8),), -0.2, 0.2)), 0.5, 4.0)
    eigen_y = jnp.clip(jnp.exp(math.log(4.0) - 2.0794415 * jax.random.uniform(keys[11], (NY,), jnp.float32) ** steps_of(keys[11], (NY,), ((0, 4),), -0.2, 0.2)), 0.5, 4.0)
    mode_shift = jnp.clip(jnp.exp(jax.random.uniform(keys[12], (MODES,), jnp.float32, math.log(0.5), math.log(2.0))), 0.5, 2.0)
    return dict(u_flow=u_flow, v_flow=v_flow, sea_mask=sea_mask, bottom_level=bottom_level, mode_project=mode_project, mode_shape=mode_shape, forward_x=forward_x, forward_y=forward_y, inverse_x=inverse_x, inverse_y=inverse_y, eigen_x=eigen_x, eigen_y=eigen_y, mode_shift=mode_shift)


def shifted_y(field, step):
    padded = jnp.pad(field, ((0, 0), (0, 0), (1, 1)))
    if step > 0:
        return padded[:, :, 2:]
    return padded[:, :, :-2]


def reference(u_flow, v_flow, sea_mask, bottom_level, mode_project, mode_shape, forward_x, forward_y, inverse_x, inverse_y, eigen_x, eigen_y, mode_shift):
    high = lax.Precision.HIGHEST
    mask_f = sea_mask.astype(jnp.float32)
    level_ids = jnp.arange(LEV, dtype=jnp.int32)

    def project(carry, inputs):
        acc_u, acc_v = carry
        u_level, v_level, weights, level = inputs
        wet = mask_f * (level < bottom_level).astype(jnp.float32)
        w32 = weights.astype(jnp.float32)[:, None, None]
        acc_u = acc_u + w32 * (wet * u_level.astype(jnp.float32))[None]
        acc_v = acc_v + w32 * (wet * v_level.astype(jnp.float32))[None]
        return (acc_u, acc_v), None

    zeros = jnp.zeros((MODES, NX, NY), jnp.float32)
    (flux_u, flux_v), _ = lax.scan(project, (zeros, zeros), (u_flow, v_flow, mode_project, level_ids))
    flux_u = flux_u.astype(jnp.bfloat16).astype(jnp.float32)
    flux_v = flux_v.astype(jnp.bfloat16).astype(jnp.float32)
    divergence = mask_f[None] * (0.5 * (jnp.roll(flux_u, -1, 1) - jnp.roll(flux_u, 1, 1)) + 0.5 * (shifted_y(flux_v, 1) - shifted_y(flux_v, -1)))
    divergence = divergence.astype(jnp.bfloat16)
    spec_x = jnp.einsum('ki,mij->mkj', forward_x.astype(jnp.float32), divergence.astype(jnp.float32), precision=high).astype(jnp.bfloat16)
    spec_xy = jnp.einsum('qj,mkj->mkq', forward_y.astype(jnp.float32), spec_x.astype(jnp.float32), precision=high)
    denom = eigen_x[None, :, None] + eigen_y[None, None, :] + mode_shift[:, None, None]
    scaled = (spec_xy / denom).astype(jnp.bfloat16)
    back_y = jnp.einsum('jq,mkq->mkj', inverse_y.astype(jnp.float32), scaled.astype(jnp.float32), precision=high).astype(jnp.bfloat16)
    pressure = jnp.einsum('ik,mkj->mij', inverse_x.astype(jnp.float32), back_y.astype(jnp.float32), precision=high)
    grad_x = 0.5 * (jnp.roll(pressure, -1, 1) - jnp.roll(pressure, 1, 1))
    grad_y = 0.5 * (shifted_y(pressure, 1) - shifted_y(pressure, -1))

    def rebuild(inputs):
        shape_row, level = inputs
        wet = mask_f * (level < bottom_level).astype(jnp.float32)
        corr_u = -wet * (shape_row[0] * grad_x[0] + shape_row[1] * grad_x[1])
        corr_v = -wet * (shape_row[0] * grad_y[0] + shape_row[1] * grad_y[1])
        return corr_u.astype(jnp.bfloat16), corr_v.astype(jnp.bfloat16)

    u_correct, v_correct = lax.map(rebuild, (mode_shape, level_ids))
    return u_correct, v_correct, pressure
```

```python
import functools

import jax
import jax.numpy as jnp
from jax import lax
from jax.experimental import pallas as pl
from jax.experimental.pallas import tpu as pltpu
from jax.sharding import PartitionSpec as P

F32, BF16 = jnp.float32, jnp.bfloat16
ROWS = 16
PAD = 8
MESH = pl.DeviceIdType.MESH
LAST = (((1,), (1,)), ((), ()))


def remote(src, dst, send, recv, **device):
    return pltpu.make_async_remote_copy(
        src_ref=src, dst_ref=dst, send_sem=send, recv_sem=recv, device_id=device, device_id_type=MESH
    )


def gather_x(n, rows, buf, across_send, across_recv, pair_send, pair_recv):
    me = lax.axis_index("gx")
    chips = n // 2
    chip, core = me // 2, me % 2
    other = chip * 2 + 1 - core

    def block(device):
        return buf.at[pl.ds(pl.multiple_of(device * rows, ROWS), rows)]

    across, pair = [], []
    for d in range(1, chips):
        target = ((chip + d) % chips) * 2 + core
        copy = remote(block(me), block(me), across_send.at[d], across_recv.at[d], gx=target)
        copy.start()
        across.append(copy)
    copy = remote(block(me), block(me), pair_send.at[0], pair_recv.at[0], gx=other)
    copy.start()
    pair.append(copy)
    for d in range(1, chips):
        source = ((chip - d + chips) % chips) * 2 + core
        across[d - 1].wait_recv()
        copy = remote(block(source), block(source), pair_send.at[d], pair_recv.at[d], gx=other)
        copy.start()
        pair.append(copy)
    for copy in pair:
        copy.wait_recv()
    return across + pair


def gather_y(p, width, src, buf, send, recv):
    me = lax.axis_index("gy")
    columns = pl.ds(pl.multiple_of(me * width, width), width)
    copies = []
    for d in range(1, p):
        copy = remote(src, buf.at[:, columns], send.at[d], recv.at[d], gy=(me + d) % p)
        copy.start()
        copies.append(copy)
    buf[:, columns] = src[...]
    for copy in copies:
        copy.wait_recv()
    return copies


def kernel(
    n, p, u_ref, v_ref, sea_ref, bottom_ref, project_ref, fx_ref, fy_ref, ix_ref, iy_ref, ex_ref, ey_ref,
    shape_ref, shift_ref, uc_ref, vc_ref, p_ref,
    weights, fu, fv, xsend, xrecv, ysend, yrecv, xg, xg2, ysrc, ysrc2, yg, yg2, ixe, pp, grad, psend, precv, denom,
    edge_s, edge_r, ye_s, ye_r, pe_s, pe_r, as1, ar1, ps1, pr1, as2, ar2, ps2, pr2, ys1, yr1, ys2, yr2,
):
    levels, rows, width = u_ref.shape
    me_x, me_y = lax.axis_index("gx"), lax.axis_index("gy")
    left, right = (me_x + n - 1) % n, (me_x + 1) % n
    barrier = pltpu.get_barrier_semaphore()
    for d in range(1, n):
        pl.semaphore_signal(barrier, inc=1, device_id={"gx": (me_x + d) % n}, device_id_type=MESH)
    for d in range(1, p):
        pl.semaphore_signal(barrier, inc=1, device_id={"gy": (me_y + d) % p}, device_id_type=MESH)

    table = project_ref[...].astype(F32)
    for level in range(levels):
        for mode in range(2):
            weights[2 * level + mode] = jnp.broadcast_to(
                table[level : level + 1, mode : mode + 1], (ROWS, width)
            )

    def depth_of(at):
        return jnp.where(sea_ref[at, :] > 0, bottom_ref[at, :], 0)

    def project(ref, out, pad, step):
        at = pl.ds(pl.multiple_of(step * ROWS, ROWS), ROWS)
        depth = depth_of(at)
        sums = [jnp.zeros((ROWS, width), F32)] * 2
        for level in range(levels):
            value = jnp.where(level < depth, ref[level, at, :].astype(F32), 0.0)
            for mode in range(2):
                sums[mode] = sums[mode] + weights[2 * level + mode] * value
        to = pl.ds(pl.multiple_of(step * ROWS + pad, 8), ROWS)
        for mode in range(2):
            out[mode, to, :] = sums[mode].astype(BF16).astype(F32)

    def edges(first, second, out):
        lane = lax.broadcasted_iota(jnp.int32, (rows, width), 1)
        out[0] = jnp.where(lane == 0, first, pltpu.roll(second, 1, 1)).astype(BF16)
        out[1] = jnp.where(lane == width - 1, first, pltpu.roll(second, width - 1, 1)).astype(BF16)

    def swap_y(src, dst, send, recv, act):
        down = remote(src.at[0], dst.at[1], send.at[0], recv.at[1], gy=jnp.maximum(me_y - 1, 0))
        up = remote(src.at[1], dst.at[0], send.at[1], recv.at[0], gy=jnp.minimum(me_y + 1, p - 1))

        @pl.when(me_y > 0)
        def _():
            if act == "start":
                down.start()
            if act == "send":
                down.wait_send()
            if act == "recv":
                up.wait_recv()

        @pl.when(me_y < p - 1)
        def _():
            if act == "start":
                up.start()
            if act == "send":
                up.wait_send()
            if act == "recv":
                down.wait_recv()

    def difference_y(field, halo, mode):
        lane = lax.broadcasted_iota(jnp.int32, (rows, width), 1)
        low, high = halo[0].astype(F32), halo[1].astype(F32)
        before = jnp.where(lane == 0, pltpu.roll(low, 1 + mode, 1), pltpu.roll(field, 1, 1))
        after = jnp.where(
            lane == width - 1, pltpu.roll(high, width - 1 - mode, 1), pltpu.roll(field, width - 1, 1)
        )
        return 0.5 * (after - before)

    @pl.when(me_y == 0)
    def _():
        yrecv[0] = jnp.zeros((rows, width), BF16)
        precv[0] = jnp.zeros((rows, width), BF16)

    @pl.when(me_y == p - 1)
    def _():
        yrecv[1] = jnp.zeros((rows, width), BF16)
        precv[1] = jnp.zeros((rows, width), BF16)

    steps = rows // ROWS
    project(u_ref, fu, PAD, 0)
    project(u_ref, fu, PAD, steps - 1)
    xsend[...] = jnp.zeros(xsend.shape, F32)
    for mode in range(2):
        xsend[0, mode : mode + 1, :] = fu[mode, PAD : PAD + 1, :]
        xsend[1, mode : mode + 1, :] = fu[mode, PAD + rows - 1 : PAD + rows, :]

    pl.semaphore_wait(barrier, n - 1 + p - 1)
    to_left = remote(xsend.at[0], xrecv.at[1], edge_s.at[0], edge_r.at[0], gx=left)
    to_right = remote(xsend.at[1], xrecv.at[0], edge_s.at[1], edge_r.at[1], gx=right)
    to_left.start()
    to_right.start()

    def project_v(step, carry):
        project(v_ref, fv, 0, step)
        return carry

    def project_u(step, carry):
        project(u_ref, fu, PAD, step)
        return carry

    lax.fori_loop(0, steps, project_v, 0)
    edges(fv[0], fv[1], ysend)
    swap_y(ysend, yrecv, ye_s, ye_r, "start")
    lax.fori_loop(1, steps - 1, project_u, 0)

    to_left.wait_recv()
    to_right.wait_recv()
    for mode in range(2):
        fu[mode, PAD - 1 : PAD, :] = xrecv[0, mode : mode + 1, :]
        fu[mode, PAD + rows : PAD + rows + 1, :] = xrecv[1, mode : mode + 1, :]
    swap_y(ysend, yrecv, ye_s, ye_r, "recv")
    sea = sea_ref[...].astype(F32)
    mine = pl.ds(pl.multiple_of(me_x * rows, ROWS), rows)
    for mode in range(2):
        along_x = 0.5 * (
            fu[mode, PAD + 1 : PAD + 1 + rows, :] - fu[mode, PAD - 1 : PAD - 1 + rows, :]
        )
        along_y = difference_y(fv[mode], yrecv, mode)
        xg[mine, mode * width : (mode + 1) * width] = (sea * (along_x + along_y)).astype(BF16)
    sent = gather_x(n, rows, xg, as1, ar1, ps1, pr1)

    rows_left = remote(ix_ref.at[0:ROWS], ixe.at[ROWS : 2 * ROWS], edge_s.at[2], edge_r.at[2], gx=left)
    rows_right = remote(
        ix_ref.at[rows - ROWS : rows], ixe.at[0:ROWS], edge_s.at[3], edge_r.at[3], gx=right
    )
    rows_left.start()
    rows_right.start()
    spectrum = jnp.dot(fx_ref[...], xg[...], preferred_element_type=F32)
    for mode in range(2):
        ysrc[mode * rows : (mode + 1) * rows, :] = spectrum[:, mode * width : (mode + 1) * width].astype(BF16)
    row = lax.broadcasted_iota(jnp.int32, (rows, rows), 0)
    column = lax.broadcasted_iota(jnp.int32, (rows, rows), 1)
    ex = jnp.sum(jnp.where(row == column, ex_ref[...], 0.0), axis=1, keepdims=True)
    for mode in range(2):
        denom[mode * rows : (mode + 1) * rows, :] = ex + ey_ref[...] + shift_ref[mode]
    sent += gather_y(p, width, ysrc, yg, ys1, yr1)
    spectrum = lax.dot_general(yg[...], fy_ref[...], LAST, preferred_element_type=F32)
    ysrc2[...] = (spectrum / denom[...]).astype(BF16)
    sent += gather_y(p, width, ysrc2, yg2, ys2, yr2)
    back = lax.dot_general(yg2[...], iy_ref[...], LAST, preferred_element_type=F32).astype(BF16)
    for mode in range(2):
        xg2[mine, mode * width : (mode + 1) * width] = back[mode * rows : (mode + 1) * rows]
    sent += gather_x(n, rows, xg2, as2, ar2, ps2, pr2)

    pressure = jnp.dot(ix_ref[...], xg2[...], preferred_element_type=F32)
    fields = [pressure[:, mode * width : (mode + 1) * width] for mode in range(2)]
    edges(fields[0], fields[1], psend)
    swap_y(psend, precv, pe_s, pe_r, "start")
    for mode in range(2):
        p_ref[mode] = fields[mode]
        pp[mode, PAD : PAD + rows, :] = fields[mode]
    rows_left.wait_recv()
    rows_right.wait_recv()
    outside = jnp.dot(ixe[...], xg2[...], preferred_element_type=F32)
    for mode in range(2):
        part = outside[:, mode * width : (mode + 1) * width]
        pp[mode, PAD - 1 : PAD, :] = part[ROWS - 1 : ROWS]
        pp[mode, PAD + rows : PAD + rows + 1, :] = part[ROWS : ROWS + 1]
    for mode in range(2):
        grad[mode] = 0.5 * (
            pp[mode, PAD + 1 : PAD + 1 + rows, :] - pp[mode, PAD - 1 : PAD - 1 + rows, :]
        )

    def rebuild(out):
        def one(step, carry):
            at = pl.ds(pl.multiple_of(step * ROWS, ROWS), ROWS)
            depth = depth_of(at)
            zero, one = grad[0, at, :], grad[1, at, :]
            for level in range(levels):
                value = -(shape_ref[level, 0] * zero + shape_ref[level, 1] * one)
                out[level, at, :] = jnp.where(level < depth, value, 0.0).astype(BF16)
            return carry

        lax.fori_loop(0, steps, one, 0)

    rebuild(uc_ref)
    swap_y(psend, precv, pe_s, pe_r, "recv")
    for mode in range(2):
        grad[mode] = difference_y(p_ref[mode], precv, mode)
    rebuild(vc_ref)

    for copy in sent + [to_left, to_right, rows_left, rows_right]:
        copy.wait_send()
    swap_y(ysend, yrecv, ye_s, ye_r, "send")
    swap_y(psend, precv, pe_s, pe_r, "send")


def body(
    n,
    p,
    u_flow,
    v_flow,
    sea_mask,
    bottom_level,
    mode_project,
    mode_shape,
    forward_x,
    forward_y,
    inverse_x,
    inverse_y,
    eigen_x,
    eigen_y,
    mode_shift,
):
    levels, rows, width = u_flow.shape
    nx, ny = n * rows, p * width
    vmem = pl.BlockSpec(memory_space=pltpu.VMEM)
    smem = pl.BlockSpec(memory_space=pltpu.SMEM)
    dma = pltpu.SemaphoreType.DMA
    chips = n // 2
    return pl.pallas_call(
        functools.partial(kernel, n, p),
        out_shape=(
            jax.ShapeDtypeStruct(u_flow.shape, BF16),
            jax.ShapeDtypeStruct(v_flow.shape, BF16),
            jax.ShapeDtypeStruct((2, rows, width), F32),
        ),
        in_specs=[vmem] * 11 + [smem] * 2,
        out_specs=(vmem,) * 3,
        scratch_shapes=[
            pltpu.VMEM((2 * levels, ROWS, width), F32),
            pltpu.VMEM((2, rows + 2 * PAD, width), F32),
            pltpu.VMEM((2, rows, width), F32),
            pltpu.VMEM((2, 8, width), F32),
            pltpu.VMEM((2, 8, width), F32),
            pltpu.VMEM((2, rows, width), BF16),
            pltpu.VMEM((2, rows, width), BF16),
            pltpu.VMEM((nx, 2 * width), BF16),
            pltpu.VMEM((nx, 2 * width), BF16),
            pltpu.VMEM((2 * rows, width), BF16),
            pltpu.VMEM((2 * rows, width), BF16),
            pltpu.VMEM((2 * rows, ny), BF16),
            pltpu.VMEM((2 * rows, ny), BF16),
            pltpu.VMEM((2 * ROWS, nx), BF16),
            pltpu.VMEM((2, rows + 2 * PAD, width), F32),
            pltpu.VMEM((2, rows, width), F32),
            pltpu.VMEM((2, rows, width), BF16),
            pltpu.VMEM((2, rows, width), BF16),
            pltpu.VMEM((2 * rows, width), F32),
            dma((4,)),
            dma((4,)),
            dma((2,)),
            dma((2,)),
            dma((2,)),
            dma((2,)),
        ]
        + [dma((chips,))] * 8
        + [dma((p,))] * 4,
        compiler_params=pltpu.CompilerParams(
            collective_id=0, has_side_effects=True, vmem_limit_bytes=56 * 2**20
        ),
        cost_estimate=pl.CostEstimate(
            flops=8 * rows * width * (nx + ny), bytes_accessed=8 * u_flow.size, transcendentals=0
        ),
    )(
        u_flow,
        v_flow,
        sea_mask,
        bottom_level,
        mode_project,
        forward_x,
        forward_y,
        inverse_x,
        inverse_y,
        eigen_x[None],
        eigen_y[None],
        mode_shape,
        mode_shift,
    )


def solution(mesh):
    return jax.shard_map(
        functools.partial(body, mesh.shape["gx"], mesh.shape["gy"]),
        mesh=mesh,
        in_specs=(
            P(None, "gx", "gy"),
            P(None, "gx", "gy"),
            P("gx", "gy"),
            P("gx", "gy"),
            P(),
            P(),
            P("gx", None),
            P("gy", None),
            P("gx", None),
            P("gy", None),
            P("gx"),
            P("gy"),
            P(),
        ),
        out_specs=(P(None, "gx", "gy"), P(None, "gx", "gy"), P(None, "gx", "gy")),
        check_vma=False,
    )
```

```python
import functools

import jax
import jax.numpy as jnp
from jax import lax
from jax.experimental import pallas as pl
from jax.experimental.pallas import tpu as pltpu
from jax.sharding import PartitionSpec as P

F32, BF16 = jnp.float32, jnp.bfloat16
ROWS = 16
PAD = 8
MESH = pl.DeviceIdType.MESH
LAST = (((1,), (1,)), ((), ()))


def remote(src, dst, send, recv, **device):
    return pltpu.make_async_remote_copy(
        src_ref=src, dst_ref=dst, send_sem=send, recv_sem=recv, device_id=device, device_id_type=MESH
    )


class AcrossX:
    def __init__(self, n, rows, buf, across_send, across_recv, pair_send, pair_recv):
        me = lax.axis_index("gx")
        chips = n // 2
        chip, core = me // 2, me % 2
        other = chip * 2 + 1 - core

        def block(device):
            return buf.at[pl.ds(pl.multiple_of(device * rows, ROWS), rows)]

        self.across, self.pair = [], []
        for d in range(chips):
            source = ((chip - d + chips) % chips) * 2 + core
            target = ((chip + d) % chips) * 2 + core
            self.pair.append(remote(block(source), block(source), pair_send.at[d], pair_recv.at[d], gx=other))
            if d > 0:
                self.across.append(
                    remote(block(me), block(me), across_send.at[d], across_recv.at[d], gx=target)
                )

    def start(self):
        for copy in self.across:
            copy.start()
        self.pair[0].start()

    def finish(self):
        for arrival, onward in zip(self.across, self.pair[1:]):
            arrival.wait_recv()
            onward.start()
        for copy in self.pair:
            copy.wait_recv()

    def wait_send(self):
        for copy in self.across + self.pair:
            copy.wait_send()


class AcrossY:
    def __init__(self, p, width, src, buf, send, recv):
        me = lax.axis_index("gy")
        columns = pl.ds(pl.multiple_of(me * width, width), width)
        self.own = (src, buf, columns)
        self.copies = [
            remote(src, buf.at[:, columns], send.at[d], recv.at[d], gy=(me + d) % p) for d in range(1, p)
        ]

    def start(self):
        src, buf, columns = self.own
        for copy in self.copies:
            copy.start()
        buf[:, columns] = src[...]

    def finish(self):
        for copy in self.copies:
            copy.wait_recv()

    def wait_send(self):
        for copy in self.copies:
            copy.wait_send()


def depth_of(sea_ref, bottom_ref, at):
    return jnp.where(sea_ref[at, :] > 0, bottom_ref[at, :], 0)


def rebuild_kernel(gx_ref, gy_ref, pressure_ref, sea_ref, bottom_ref, shape_ref, uc_ref, vc_ref, p_ref):
    levels, rows, _ = uc_ref.shape
    p_ref[...] = pressure_ref[...]

    def one(step, carry):
        at = pl.ds(pl.multiple_of(step * ROWS, ROWS), ROWS)
        depth = depth_of(sea_ref, bottom_ref, at)
        for grad, out in ((gx_ref, uc_ref), (gy_ref, vc_ref)):
            first, second = grad[0, at, :], grad[1, at, :]
            for level in range(levels):
                value = -(shape_ref[0, level] * first + shape_ref[1, level] * second)
                out[level, at, :] = jnp.where(level < depth, value, 0.0).astype(BF16)
        return carry

    lax.fori_loop(0, rows // ROWS, one, 0)


def kernel(
    n, p, u_hbm, v_hbm, sea_hbm, bottom_hbm, fx_hbm, fy_hbm, ix_hbm, iy_hbm, project_ref, ex_ref, ey_ref,
    shift_ref, gx_ref, gy_ref, p_ref,
    u_ref, v_ref, sea_ref, bottom_ref, fx_ref, fy_ref, ix_ref, iy_ref, loaded,
    weights, fu, fv, xsend, xrecv, ysend, yrecv, xg, xg2, ysrc, ysrc2, yg, yg2, ixe, pp, psend, precv, denom,
    edge_s, edge_r, ye_s, ye_r, pe_s, pe_r, as1, ar1, ps1, pr1, as2, ar2, ps2, pr2, ys1, yr1, ys2, yr2,
):
    levels, rows, width = u_ref.shape
    pairs = (
        (sea_hbm, sea_ref),
        (bottom_hbm, bottom_ref),
        (u_hbm, u_ref),
        (v_hbm, v_ref),
        (ix_hbm, ix_ref),
        (fx_hbm, fx_ref),
        (fy_hbm, fy_ref),
        (iy_hbm, iy_ref),
    )
    loads = [pltpu.make_async_copy(src, dst, loaded.at[i]) for i, (src, dst) in enumerate(pairs)]
    for load in loads:
        load.start()
    me_x, me_y = lax.axis_index("gx"), lax.axis_index("gy")
    left, right = (me_x + n - 1) % n, (me_x + 1) % n
    barrier = pltpu.get_barrier_semaphore()
    for d in range(1, n):
        pl.semaphore_signal(barrier, inc=1, device_id={"gx": (me_x + d) % n}, device_id_type=MESH)
    for d in range(1, p):
        pl.semaphore_signal(barrier, inc=1, device_id={"gy": (me_y + d) % p}, device_id_type=MESH)

    table = project_ref[...].astype(F32)
    for level in range(levels):
        for mode in range(2):
            weights[2 * level + mode] = jnp.broadcast_to(
                table[mode : mode + 1, level : level + 1], (ROWS, width)
            )

    def project(ref, out, pad, step):
        at = pl.ds(pl.multiple_of(step * ROWS, ROWS), ROWS)
        depth = depth_of(sea_ref, bottom_ref, at)
        sums = [jnp.zeros((ROWS, width), F32)] * 2
        for level in range(levels):
            value = jnp.where(level < depth, ref[level, at, :].astype(F32), 0.0)
            for mode in range(2):
                sums[mode] = sums[mode] + weights[2 * level + mode] * value
        to = pl.ds(pl.multiple_of(step * ROWS + pad, 8), ROWS)
        for mode in range(2):
            out[mode, to, :] = sums[mode].astype(BF16).astype(F32)

    def edges(first, second, out):
        lane = lax.broadcasted_iota(jnp.int32, (rows, width), 1)
        out[0] = jnp.where(lane == 0, first, pltpu.roll(second, 1, 1)).astype(BF16)
        out[1] = jnp.where(lane == width - 1, first, pltpu.roll(second, width - 1, 1)).astype(BF16)

    def swap_y(src, dst, send, recv, act):
        down = remote(src.at[0], dst.at[1], send.at[0], recv.at[1], gy=jnp.maximum(me_y - 1, 0))
        up = remote(src.at[1], dst.at[0], send.at[1], recv.at[0], gy=jnp.minimum(me_y + 1, p - 1))

        @pl.when(me_y > 0)
        def _():
            if act == "start":
                down.start()
            if act == "send":
                down.wait_send()
            if act == "recv":
                up.wait_recv()

        @pl.when(me_y < p - 1)
        def _():
            if act == "start":
                up.start()
            if act == "send":
                up.wait_send()
            if act == "recv":
                down.wait_recv()

    def difference_y(field, halo, mode):
        lane = lax.broadcasted_iota(jnp.int32, (rows, width), 1)
        low, high = halo[0].astype(F32), halo[1].astype(F32)
        before = jnp.where(lane == 0, pltpu.roll(low, 1 + mode, 1), pltpu.roll(field, 1, 1))
        after = jnp.where(
            lane == width - 1, pltpu.roll(high, width - 1 - mode, 1), pltpu.roll(field, width - 1, 1)
        )
        return 0.5 * (after - before)

    @pl.when(me_y == 0)
    def _():
        yrecv[0] = jnp.zeros((rows, width), BF16)
        precv[0] = jnp.zeros((rows, width), BF16)

    @pl.when(me_y == p - 1)
    def _():
        yrecv[1] = jnp.zeros((rows, width), BF16)
        precv[1] = jnp.zeros((rows, width), BF16)

    steps = rows // ROWS
    for load in loads[:3]:
        load.wait()
    project(u_ref, fu, PAD, 0)
    project(u_ref, fu, PAD, steps - 1)
    xsend[...] = jnp.zeros(xsend.shape, F32)
    for mode in range(2):
        xsend[0, mode : mode + 1, :] = fu[mode, PAD : PAD + 1, :]
        xsend[1, mode : mode + 1, :] = fu[mode, PAD + rows - 1 : PAD + rows, :]

    pl.semaphore_wait(barrier, n - 1 + p - 1)
    to_left = remote(xsend.at[0], xrecv.at[1], edge_s.at[0], edge_r.at[0], gx=left)
    to_right = remote(xsend.at[1], xrecv.at[0], edge_s.at[1], edge_r.at[1], gx=right)
    to_left.start()
    to_right.start()

    def project_v(step, carry):
        project(v_ref, fv, 0, step)
        return carry

    def project_u(step, carry):
        project(u_ref, fu, PAD, step)
        return carry

    loads[3].wait()
    lax.fori_loop(0, steps, project_v, 0)
    edges(fv[0], fv[1], ysend)
    swap_y(ysend, yrecv, ye_s, ye_r, "start")
    lax.fori_loop(1, steps - 1, project_u, 0)

    to_left.wait_recv()
    to_right.wait_recv()
    for mode in range(2):
        fu[mode, PAD - 1 : PAD, :] = xrecv[0, mode : mode + 1, :]
        fu[mode, PAD + rows : PAD + rows + 1, :] = xrecv[1, mode : mode + 1, :]
    swap_y(ysend, yrecv, ye_s, ye_r, "recv")
    sea = sea_ref[...].astype(F32)
    mine = pl.ds(pl.multiple_of(me_x * rows, ROWS), rows)
    modes = range(2)
    gx1 = [AcrossX(n, rows, xg.at[m], as1.at[m], ar1.at[m], ps1.at[m], pr1.at[m]) for m in modes]
    gx2 = [AcrossX(n, rows, xg2.at[m], as2.at[m], ar2.at[m], ps2.at[m], pr2.at[m]) for m in modes]
    gy1 = [AcrossY(p, width, ysrc.at[m], yg.at[m], ys1.at[m], yr1.at[m]) for m in modes]
    gy2 = [AcrossY(p, width, ysrc2.at[m], yg2.at[m], ys2.at[m], yr2.at[m]) for m in modes]
    for mode in modes:
        along_x = 0.5 * (
            fu[mode, PAD + 1 : PAD + 1 + rows, :] - fu[mode, PAD - 1 : PAD - 1 + rows, :]
        )
        along_y = difference_y(fv[mode], yrecv, mode)
        xg[mode, mine, :] = (sea * (along_x + along_y)).astype(BF16)
        gx1[mode].start()

    for load in loads[4:]:
        load.wait()
    rows_left = remote(ix_ref.at[0:ROWS], ixe.at[ROWS : 2 * ROWS], edge_s.at[2], edge_r.at[2], gx=left)
    rows_right = remote(
        ix_ref.at[rows - ROWS : rows], ixe.at[0:ROWS], edge_s.at[3], edge_r.at[3], gx=right
    )
    rows_left.start()
    rows_right.start()
    row = lax.broadcasted_iota(jnp.int32, (rows, rows), 0)
    column = lax.broadcasted_iota(jnp.int32, (rows, rows), 1)
    ex = jnp.sum(jnp.where(row == column, ex_ref[...], 0.0), axis=1, keepdims=True)
    for mode in modes:
        denom[mode] = ex + ey_ref[...] + shift_ref[mode]
    for mode in modes:
        gx1[mode].finish()
        ysrc[mode] = jnp.dot(fx_ref[...], xg[mode], preferred_element_type=F32).astype(BF16)
        gy1[mode].start()
    for mode in modes:
        gy1[mode].finish()
        spectrum = lax.dot_general(yg[mode], fy_ref[...], LAST, preferred_element_type=F32)
        ysrc2[mode] = (spectrum / denom[mode]).astype(BF16)
        gy2[mode].start()
    for mode in modes:
        gy2[mode].finish()
        back = lax.dot_general(yg2[mode], iy_ref[...], LAST, preferred_element_type=F32)
        xg2[mode, mine, :] = back.astype(BF16)
        gx2[mode].start()
    rows_left.wait_recv()
    rows_right.wait_recv()
    for mode in modes:
        gx2[mode].finish()
        field = jnp.dot(ix_ref[...], xg2[mode], preferred_element_type=F32)
        p_ref[mode] = field
        pp[mode, PAD : PAD + rows, :] = field
    edges(p_ref[0], p_ref[1], psend)
    swap_y(psend, precv, pe_s, pe_r, "start")
    for mode in modes:
        outside = jnp.dot(ixe[...], xg2[mode], preferred_element_type=F32)
        pp[mode, PAD - 1 : PAD, :] = outside[ROWS - 1 : ROWS]
        pp[mode, PAD + rows : PAD + rows + 1, :] = outside[ROWS : ROWS + 1]
        gx_ref[mode] = 0.5 * (
            pp[mode, PAD + 1 : PAD + 1 + rows, :] - pp[mode, PAD - 1 : PAD - 1 + rows, :]
        )
    for copy in gx1 + gx2 + gy1 + gy2 + [to_left, to_right, rows_left, rows_right]:
        copy.wait_send()
    swap_y(ysend, yrecv, ye_s, ye_r, "send")
    swap_y(psend, precv, pe_s, pe_r, "recv")
    for mode in modes:
        gy_ref[mode] = difference_y(p_ref[mode], precv, mode)
    swap_y(psend, precv, pe_s, pe_r, "send")


def body(
    n,
    p,
    u_flow,
    v_flow,
    sea_mask,
    bottom_level,
    mode_project,
    mode_shape,
    forward_x,
    forward_y,
    inverse_x,
    inverse_y,
    eigen_x,
    eigen_y,
    mode_shift,
):
    levels, rows, width = u_flow.shape
    nx, ny = n * rows, p * width
    vmem = pl.BlockSpec(memory_space=pltpu.VMEM)
    smem = pl.BlockSpec(memory_space=pltpu.SMEM)
    dma = pltpu.SemaphoreType.DMA
    chips = n // 2
    field = jax.ShapeDtypeStruct((2, rows, width), F32)
    grad_x, grad_y, pressure = pl.pallas_call(
        functools.partial(kernel, n, p),
        out_shape=(field,) * 3,
        in_specs=[pl.BlockSpec(memory_space=pl.ANY)] * 8 + [vmem] * 3 + [smem],
        out_specs=(vmem,) * 3,
        scratch_shapes=[
            pltpu.VMEM(source.shape, source.dtype)
            for source in (
                u_flow, v_flow, sea_mask, bottom_level, forward_x, forward_y, inverse_x, inverse_y
            )
        ]
        + [dma((8,))]
        + [
            pltpu.VMEM((2 * levels, ROWS, width), F32),
            pltpu.VMEM((2, rows + 2 * PAD, width), F32),
            pltpu.VMEM((2, rows, width), F32),
            pltpu.VMEM((2, 8, width), F32),
            pltpu.VMEM((2, 8, width), F32),
            pltpu.VMEM((2, rows, width), BF16),
            pltpu.VMEM((2, rows, width), BF16),
            pltpu.VMEM((2, nx, width), BF16),
            pltpu.VMEM((2, nx, width), BF16),
            pltpu.VMEM((2, rows, width), BF16),
            pltpu.VMEM((2, rows, width), BF16),
            pltpu.VMEM((2, rows, ny), BF16),
            pltpu.VMEM((2, rows, ny), BF16),
            pltpu.VMEM((2 * ROWS, nx), BF16),
            pltpu.VMEM((2, rows + 2 * PAD, width), F32),
            pltpu.VMEM((2, rows, width), BF16),
            pltpu.VMEM((2, rows, width), BF16),
            pltpu.VMEM((2, rows, width), F32),
            dma((4,)),
            dma((4,)),
            dma((2,)),
            dma((2,)),
            dma((2,)),
            dma((2,)),
        ]
        + [dma((2, chips))] * 8
        + [dma((2, p))] * 4,
        compiler_params=pltpu.CompilerParams(
            collective_id=0, has_side_effects=True, vmem_limit_bytes=56 * 2**20
        ),
        cost_estimate=pl.CostEstimate(
            flops=8 * rows * width * (nx + ny), bytes_accessed=8 * u_flow.size, transcendentals=0
        ),
    )(
        u_flow,
        v_flow,
        sea_mask,
        bottom_level,
        forward_x,
        forward_y,
        inverse_x,
        inverse_y,
        mode_project.T,
        eigen_x[None],
        eigen_y[None],
        mode_shift,
    )
    return pl.pallas_call(
        rebuild_kernel,
        out_shape=(
            jax.ShapeDtypeStruct(u_flow.shape, BF16),
            jax.ShapeDtypeStruct(v_flow.shape, BF16),
            field,
        ),
        in_specs=[vmem] * 5 + [smem],
        out_specs=(vmem,) * 3,
        compiler_params=pltpu.CompilerParams(vmem_limit_bytes=56 * 2**20),
        cost_estimate=pl.CostEstimate(
            flops=8 * u_flow.size, bytes_accessed=4 * u_flow.size, transcendentals=0
        ),
    )(grad_x, grad_y, pressure, sea_mask, bottom_level, mode_shape.T)


def solution(mesh):
    return jax.shard_map(
        functools.partial(body, mesh.shape["gx"], mesh.shape["gy"]),
        mesh=mesh,
        in_specs=(
            P(None, "gx", "gy"),
            P(None, "gx", "gy"),
            P("gx", "gy"),
            P("gx", "gy"),
            P(),
            P(),
            P("gx", None),
            P("gy", None),
            P("gx", None),
            P("gy", None),
            P("gx"),
            P("gy"),
            P(),
        ),
        out_specs=(P(None, "gx", "gy"), P(None, "gx", "gy"), P(None, "gx", "gy")),
        check_vma=False,
    )
```

```python
import functools

import jax
import jax.numpy as jnp
from jax import lax
from jax.experimental import pallas as pl
from jax.experimental.pallas import tpu as pltpu
from jax.sharding import PartitionSpec as P

F32, BF16 = jnp.float32, jnp.bfloat16
ROWS = 16
PAD = 8
MESH = pl.DeviceIdType.MESH
LAST = (((1,), (1,)), ((), ()))


def remote(src, dst, send, recv, **device):
    return pltpu.make_async_remote_copy(
        src_ref=src, dst_ref=dst, send_sem=send, recv_sem=recv, device_id=device, device_id_type=MESH
    )


class AcrossX:
    def __init__(self, n, rows, buf, across_send, across_recv, pair_send, pair_recv):
        me = lax.axis_index("gx")
        chips = n // 2
        chip, core = me // 2, me % 2
        other = chip * 2 + 1 - core

        def block(device):
            return buf.at[pl.ds(pl.multiple_of(device * rows, ROWS), rows)]

        self.across, self.pair = [], []
        for d in range(chips):
            source = ((chip - d + chips) % chips) * 2 + core
            target = ((chip + d) % chips) * 2 + core
            self.pair.append(remote(block(source), block(source), pair_send.at[d], pair_recv.at[d], gx=other))
            if d > 0:
                self.across.append(
                    remote(block(me), block(me), across_send.at[d], across_recv.at[d], gx=target)
                )

    def start(self):
        for copy in self.across:
            copy.start()
        self.pair[0].start()

    def finish(self):
        for arrival, onward in zip(self.across, self.pair[1:]):
            arrival.wait_recv()
            onward.start()
        for copy in self.pair:
            copy.wait_recv()

    def wait_send(self):
        for copy in self.across + self.pair:
            copy.wait_send()


class AcrossY:
    def __init__(self, p, src, buf, send, recv):
        me = lax.axis_index("gy")
        self.own = (src, buf, me)
        self.copies = [
            remote(src, buf.at[me], send.at[d], recv.at[d], gy=(me + d) % p) for d in range(1, p)
        ]

    def start(self):
        src, buf, me = self.own
        for copy in self.copies:
            copy.start()
        buf[me] = src[...]

    def finish(self):
        for copy in self.copies:
            copy.wait_recv()

    def wait_send(self):
        for copy in self.copies:
            copy.wait_send()


def depth_of(sea_ref, bottom_ref, at):
    return jnp.where(sea_ref[at, :] > 0, bottom_ref[at, :], 0)


def rebuild_kernel(gx_ref, gy_ref, pressure_ref, sea_ref, bottom_ref, shape_ref, uc_ref, vc_ref, p_ref):
    levels, rows, _ = uc_ref.shape
    p_ref[...] = pressure_ref[...]

    def one(step, carry):
        at = pl.ds(pl.multiple_of(step * ROWS, ROWS), ROWS)
        depth = depth_of(sea_ref, bottom_ref, at)
        for grad, out in ((gx_ref, uc_ref), (gy_ref, vc_ref)):
            first, second = grad[0, at, :], grad[1, at, :]
            for level in range(levels):
                value = -(shape_ref[0, level] * first + shape_ref[1, level] * second)
                out[level, at, :] = jnp.where(level < depth, value, 0.0).astype(BF16)
        return carry

    lax.fori_loop(0, rows // ROWS, one, 0)


def kernel(
    n, p, u_hbm, v_hbm, sea_hbm, bottom_hbm, fx_hbm, fy_hbm, ix_hbm, iy_hbm, project_ref, ex_ref, ey_ref,
    shift_ref, gx_ref, gy_ref, p_ref,
    u_ref, v_ref, sea_ref, bottom_ref, fx_ref, fy_ref, ix_ref, iy_ref, loaded,
    weights, fu, fv, xsend, xrecv, ysend, yrecv, xg, xg2, ysrc, ysrc2, yg, yg2, ixe, pp, psend, precv, denom,
    edge_s, edge_r, ye_s, ye_r, pe_s, pe_r, as1, ar1, ps1, pr1, as2, ar2, ps2, pr2, ys1, yr1, ys2, yr2,
):
    levels, rows, width = u_ref.shape
    pairs = (
        (sea_hbm, sea_ref),
        (bottom_hbm, bottom_ref),
        (u_hbm, u_ref),
        (v_hbm, v_ref),
        (ix_hbm, ix_ref),
        (fx_hbm, fx_ref),
        (fy_hbm, fy_ref),
        (iy_hbm, iy_ref),
    )
    loads = [pltpu.make_async_copy(src, dst, loaded.at[i]) for i, (src, dst) in enumerate(pairs)]
    for load in loads:
        load.start()
    me_x, me_y = lax.axis_index("gx"), lax.axis_index("gy")
    left, right = (me_x + n - 1) % n, (me_x + 1) % n
    barrier = pltpu.get_barrier_semaphore()
    for d in range(1, n):
        pl.semaphore_signal(barrier, inc=1, device_id={"gx": (me_x + d) % n}, device_id_type=MESH)
    for d in range(1, p):
        pl.semaphore_signal(barrier, inc=1, device_id={"gy": (me_y + d) % p}, device_id_type=MESH)

    table = project_ref[...].astype(F32)
    for level in range(levels):
        for mode in range(2):
            weights[2 * level + mode] = jnp.broadcast_to(
                table[mode : mode + 1, level : level + 1], (ROWS, width)
            )

    def project(ref, out, pad, step):
        at = pl.ds(pl.multiple_of(step * ROWS, ROWS), ROWS)
        depth = depth_of(sea_ref, bottom_ref, at)
        sums = [jnp.zeros((ROWS, width), F32)] * 2
        for level in range(levels):
            value = jnp.where(level < depth, ref[level, at, :].astype(F32), 0.0)
            for mode in range(2):
                sums[mode] = sums[mode] + weights[2 * level + mode] * value
        to = pl.ds(pl.multiple_of(step * ROWS + pad, 8), ROWS)
        for mode in range(2):
            out[mode, to, :] = sums[mode].astype(BF16).astype(F32)

    def edges(first, second, out):
        lane = lax.broadcasted_iota(jnp.int32, (rows, width), 1)
        out[0] = jnp.where(lane == 0, first, pltpu.roll(second, 1, 1)).astype(BF16)
        out[1] = jnp.where(lane == width - 1, first, pltpu.roll(second, width - 1, 1)).astype(BF16)

    def swap_y(src, dst, send, recv, act):
        down = remote(src.at[0], dst.at[1], send.at[0], recv.at[1], gy=jnp.maximum(me_y - 1, 0))
        up = remote(src.at[1], dst.at[0], send.at[1], recv.at[0], gy=jnp.minimum(me_y + 1, p - 1))

        @pl.when(me_y > 0)
        def _():
            if act == "start":
                down.start()
            if act == "send":
                down.wait_send()
            if act == "recv":
                up.wait_recv()

        @pl.when(me_y < p - 1)
        def _():
            if act == "start":
                up.start()
            if act == "send":
                up.wait_send()
            if act == "recv":
                down.wait_recv()

    def difference_y(field, halo, mode):
        lane = lax.broadcasted_iota(jnp.int32, (rows, width), 1)
        low, high = halo[0].astype(F32), halo[1].astype(F32)
        before = jnp.where(lane == 0, pltpu.roll(low, 1 + mode, 1), pltpu.roll(field, 1, 1))
        after = jnp.where(
            lane == width - 1, pltpu.roll(high, width - 1 - mode, 1), pltpu.roll(field, width - 1, 1)
        )
        return 0.5 * (after - before)

    @pl.when(me_y == 0)
    def _():
        yrecv[0] = jnp.zeros((rows, width), BF16)
        precv[0] = jnp.zeros((rows, width), BF16)

    @pl.when(me_y == p - 1)
    def _():
        yrecv[1] = jnp.zeros((rows, width), BF16)
        precv[1] = jnp.zeros((rows, width), BF16)

    steps = rows // ROWS
    for load in loads[:3]:
        load.wait()
    project(u_ref, fu, PAD, 0)
    project(u_ref, fu, PAD, steps - 1)
    xsend[...] = jnp.zeros(xsend.shape, F32)
    for mode in range(2):
        xsend[0, mode : mode + 1, :] = fu[mode, PAD : PAD + 1, :]
        xsend[1, mode : mode + 1, :] = fu[mode, PAD + rows - 1 : PAD + rows, :]

    def project_v(step, carry):
        project(v_ref, fv, 0, step)
        return carry

    loads[3].wait()
    lax.fori_loop(0, steps, project_v, 0)
    edges(fv[0], fv[1], ysend)

    pl.semaphore_wait(barrier, n - 1 + p - 1)
    to_left = remote(xsend.at[0], xrecv.at[1], edge_s.at[0], edge_r.at[0], gx=left)
    to_right = remote(xsend.at[1], xrecv.at[0], edge_s.at[1], edge_r.at[1], gx=right)
    to_left.start()
    to_right.start()

    def project_u(step, carry):
        project(u_ref, fu, PAD, step)
        return carry

    swap_y(ysend, yrecv, ye_s, ye_r, "start")
    lax.fori_loop(1, steps - 1, project_u, 0)

    to_left.wait_recv()
    to_right.wait_recv()
    for mode in range(2):
        fu[mode, PAD - 1 : PAD, :] = xrecv[0, mode : mode + 1, :]
        fu[mode, PAD + rows : PAD + rows + 1, :] = xrecv[1, mode : mode + 1, :]
    swap_y(ysend, yrecv, ye_s, ye_r, "recv")
    sea = sea_ref[...].astype(F32)
    mine = pl.ds(pl.multiple_of(me_x * rows, ROWS), rows)
    modes = range(2)
    gx1 = [AcrossX(n, rows, xg.at[m], as1.at[m], ar1.at[m], ps1.at[m], pr1.at[m]) for m in modes]
    gx2 = [AcrossX(n, rows, xg2.at[m], as2.at[m], ar2.at[m], ps2.at[m], pr2.at[m]) for m in modes]
    gy1 = [AcrossY(p, ysrc.at[m], yg.at[m], ys1.at[m], yr1.at[m]) for m in modes]
    gy2 = [AcrossY(p, ysrc2.at[m], yg2.at[m], ys2.at[m], yr2.at[m]) for m in modes]
    for mode in modes:
        along_x = 0.5 * (
            fu[mode, PAD + 1 : PAD + 1 + rows, :] - fu[mode, PAD - 1 : PAD - 1 + rows, :]
        )
        along_y = difference_y(fv[mode], yrecv, mode)
        xg[mode, mine, :] = (sea * (along_x + along_y)).astype(BF16)
        gx1[mode].start()

    for load in loads[4:]:
        load.wait()
    rows_left = remote(ix_ref.at[0:ROWS], ixe.at[ROWS : 2 * ROWS], edge_s.at[2], edge_r.at[2], gx=left)
    rows_right = remote(
        ix_ref.at[rows - ROWS : rows], ixe.at[0:ROWS], edge_s.at[3], edge_r.at[3], gx=right
    )
    rows_left.start()
    rows_right.start()
    row = lax.broadcasted_iota(jnp.int32, (rows, rows), 0)
    column = lax.broadcasted_iota(jnp.int32, (rows, rows), 1)
    ex = jnp.sum(jnp.where(row == column, ex_ref[...], 0.0), axis=1, keepdims=True)
    for mode in modes:
        denom[mode] = ex + ey_ref[...] + shift_ref[mode]
    for mode in modes:
        gx1[mode].finish()
        ysrc[mode] = jnp.dot(fx_ref[...], xg[mode], preferred_element_type=F32).astype(BF16)
        gy1[mode].start()

    def whole(blocks, mode):
        return jnp.concatenate([blocks[mode, source] for source in range(p)], axis=1)

    for mode in modes:
        gy1[mode].finish()
        spectrum = lax.dot_general(whole(yg, mode), fy_ref[...], LAST, preferred_element_type=F32)
        ysrc2[mode] = (spectrum / denom[mode]).astype(BF16)
        gy2[mode].start()
    for mode in modes:
        gy2[mode].finish()
        back = lax.dot_general(whole(yg2, mode), iy_ref[...], LAST, preferred_element_type=F32)
        xg2[mode, mine, :] = back.astype(BF16)
        gx2[mode].start()
    rows_left.wait_recv()
    rows_right.wait_recv()
    for mode in modes:
        gx2[mode].finish()
        field = jnp.dot(ix_ref[...], xg2[mode], preferred_element_type=F32)
        p_ref[mode] = field
        pp[mode, PAD : PAD + rows, :] = field
    edges(p_ref[0], p_ref[1], psend)
    swap_y(psend, precv, pe_s, pe_r, "start")
    for mode in modes:
        outside = jnp.dot(ixe[...], xg2[mode], preferred_element_type=F32)
        pp[mode, PAD - 1 : PAD, :] = outside[ROWS - 1 : ROWS]
        pp[mode, PAD + rows : PAD + rows + 1, :] = outside[ROWS : ROWS + 1]
        gx_ref[mode] = 0.5 * (
            pp[mode, PAD + 1 : PAD + 1 + rows, :] - pp[mode, PAD - 1 : PAD - 1 + rows, :]
        )
    for copy in gx1 + gx2 + gy1 + gy2 + [to_left, to_right, rows_left, rows_right]:
        copy.wait_send()
    swap_y(ysend, yrecv, ye_s, ye_r, "send")
    swap_y(psend, precv, pe_s, pe_r, "recv")
    for mode in modes:
        gy_ref[mode] = difference_y(p_ref[mode], precv, mode)
    swap_y(psend, precv, pe_s, pe_r, "send")


def body(
    n,
    p,
    u_flow,
    v_flow,
    sea_mask,
    bottom_level,
    mode_project,
    mode_shape,
    forward_x,
    forward_y,
    inverse_x,
    inverse_y,
    eigen_x,
    eigen_y,
    mode_shift,
):
    levels, rows, width = u_flow.shape
    nx, ny = n * rows, p * width
    vmem = pl.BlockSpec(memory_space=pltpu.VMEM)
    smem = pl.BlockSpec(memory_space=pltpu.SMEM)
    dma = pltpu.SemaphoreType.DMA
    chips = n // 2
    field = jax.ShapeDtypeStruct((2, rows, width), F32)
    grad_x, grad_y, pressure = pl.pallas_call(
        functools.partial(kernel, n, p),
        out_shape=(field,) * 3,
        in_specs=[pl.BlockSpec(memory_space=pl.ANY)] * 8 + [vmem] * 3 + [smem],
        out_specs=(vmem,) * 3,
        scratch_shapes=[
            pltpu.VMEM(source.shape, source.dtype)
            for source in (
                u_flow, v_flow, sea_mask, bottom_level, forward_x, forward_y, inverse_x, inverse_y
            )
        ]
        + [dma((8,))]
        + [
            pltpu.VMEM((2 * levels, ROWS, width), F32),
            pltpu.VMEM((2, rows + 2 * PAD, width), F32),
            pltpu.VMEM((2, rows, width), F32),
            pltpu.VMEM((2, 8, width), F32),
            pltpu.VMEM((2, 8, width), F32),
            pltpu.VMEM((2, rows, width), BF16),
            pltpu.VMEM((2, rows, width), BF16),
            pltpu.VMEM((2, nx, width), BF16),
            pltpu.VMEM((2, nx, width), BF16),
            pltpu.VMEM((2, rows, width), BF16),
            pltpu.VMEM((2, rows, width), BF16),
            pltpu.VMEM((2, p, rows, width), BF16),
            pltpu.VMEM((2, p, rows, width), BF16),
            pltpu.VMEM((2 * ROWS, nx), BF16),
            pltpu.VMEM((2, rows + 2 * PAD, width), F32),
            pltpu.VMEM((2, rows, width), BF16),
            pltpu.VMEM((2, rows, width), BF16),
            pltpu.VMEM((2, rows, width), F32),
            dma((4,)),
            dma((4,)),
            dma((2,)),
            dma((2,)),
            dma((2,)),
            dma((2,)),
        ]
        + [dma((2, chips))] * 8
        + [dma((2, p))] * 4,
        compiler_params=pltpu.CompilerParams(
            collective_id=0, has_side_effects=True, vmem_limit_bytes=56 * 2**20
        ),
        cost_estimate=pl.CostEstimate(
            flops=8 * rows * width * (nx + ny), bytes_accessed=8 * u_flow.size, transcendentals=0
        ),
    )(
        u_flow,
        v_flow,
        sea_mask,
        bottom_level,
        forward_x,
        forward_y,
        inverse_x,
        inverse_y,
        mode_project.T,
        eigen_x[None],
        eigen_y[None],
        mode_shift,
    )
    return pl.pallas_call(
        rebuild_kernel,
        out_shape=(
            jax.ShapeDtypeStruct(u_flow.shape, BF16),
            jax.ShapeDtypeStruct(v_flow.shape, BF16),
            field,
        ),
        in_specs=[vmem] * 5 + [smem],
        out_specs=(vmem,) * 3,
        compiler_params=pltpu.CompilerParams(vmem_limit_bytes=56 * 2**20),
        cost_estimate=pl.CostEstimate(
            flops=8 * u_flow.size, bytes_accessed=4 * u_flow.size, transcendentals=0
        ),
    )(grad_x, grad_y, pressure, sea_mask, bottom_level, mode_shape.T)


def solution(mesh):
    return jax.shard_map(
        functools.partial(body, mesh.shape["gx"], mesh.shape["gy"]),
        mesh=mesh,
        in_specs=(
            P(None, "gx", "gy"),
            P(None, "gx", "gy"),
            P("gx", "gy"),
            P("gx", "gy"),
            P(),
            P(),
            P("gx", None),
            P("gy", None),
            P("gx", None),
            P("gy", None),
            P("gx"),
            P("gy"),
            P(),
        ),
        out_specs=(P(None, "gx", "gy"), P(None, "gx", "gy"), P(None, "gx", "gy")),
        check_vma=False,
    )
```

```python
import functools

import jax
import jax.numpy as jnp
from jax import lax
from jax.experimental import pallas as pl
from jax.experimental.pallas import tpu as pltpu
from jax.sharding import PartitionSpec as P

F32, BF16 = jnp.float32, jnp.bfloat16
ROWS = 16
PAD = 8
MESH = pl.DeviceIdType.MESH
LAST = (((1,), (1,)), ((), ()))


def remote(src, dst, send, recv, **device):
    return pltpu.make_async_remote_copy(
        src_ref=src, dst_ref=dst, send_sem=send, recv_sem=recv, device_id=device, device_id_type=MESH
    )


class AcrossX:
    def __init__(self, n, rows, buf, across_send, across_recv, pair_send, pair_recv):
        me = lax.axis_index("gx")
        chips = n // 2
        chip, core = me // 2, me % 2
        other = chip * 2 + 1 - core

        def block(device):
            return buf.at[pl.ds(pl.multiple_of(device * rows, ROWS), rows)]

        self.across, self.pair = [], []
        for d in range(chips):
            source = ((chip - d + chips) % chips) * 2 + core
            target = ((chip + d) % chips) * 2 + core
            self.pair.append(remote(block(source), block(source), pair_send.at[d], pair_recv.at[d], gx=other))
            if d > 0:
                self.across.append(
                    remote(block(me), block(me), across_send.at[d], across_recv.at[d], gx=target)
                )

    def start(self):
        for copy in self.across:
            copy.start()
        self.pair[0].start()

    def finish(self):
        for arrival, onward in zip(self.across, self.pair[1:]):
            arrival.wait_recv()
            onward.start()
        for copy in self.pair:
            copy.wait_recv()

    def wait_send(self):
        for copy in self.across + self.pair:
            copy.wait_send()


class AcrossY:
    def __init__(self, p, src, buf, send, recv):
        me = lax.axis_index("gy")
        self.own = (src, buf, me)
        self.copies = [
            remote(src, buf.at[me], send.at[d], recv.at[d], gy=(me + d) % p) for d in range(1, p)
        ]

    def start(self):
        src, buf, me = self.own
        for copy in self.copies:
            copy.start()
        buf[me] = src[...]

    def finish(self):
        for copy in self.copies:
            copy.wait_recv()

    def wait_send(self):
        for copy in self.copies:
            copy.wait_send()


def depth_of(sea_ref, bottom_ref, at):
    return jnp.where(sea_ref[at, :] > 0, bottom_ref[at, :], 0)


def rebuild_kernel(gx_ref, gy_ref, pressure_ref, sea_ref, bottom_ref, shape_ref, uc_ref, vc_ref, p_ref):
    levels, rows, _ = uc_ref.shape
    p_ref[...] = pressure_ref[...]

    def one(step, carry):
        at = pl.ds(pl.multiple_of(step * ROWS, ROWS), ROWS)
        depth = depth_of(sea_ref, bottom_ref, at)
        for grad, out in ((gx_ref, uc_ref), (gy_ref, vc_ref)):
            first, second = grad[0, at, :], grad[1, at, :]
            for level in range(levels):
                value = -(shape_ref[0, level] * first + shape_ref[1, level] * second)
                out[level, at, :] = jnp.where(level < depth, value, 0.0).astype(BF16)
        return carry

    lax.fori_loop(0, rows // ROWS, one, 0)


def kernel(
    n, p, u_hbm, v_hbm, sea_hbm, bottom_hbm, fx_hbm, fy_hbm, ix_hbm, iy_hbm, project_ref, ex_ref, ey_ref,
    shift_ref, gx_ref, gy_ref, p_ref,
    u_ref, v_ref, sea_ref, bottom_ref, fx_ref, fy_ref, ix_ref, iy_ref, loaded,
    weights, fu, fv, xsend, xrecv, ysend, yrecv, xg, xg2, ysrc, ysrc2, yg, yg2, ixe, pp, psend, precv, denom,
    edge_s, edge_r, ye_s, ye_r, pe_s, pe_r, as1, ar1, ps1, pr1, as2, ar2, ps2, pr2, ys1, yr1, ys2, yr2,
):
    levels, rows, width = u_ref.shape
    pairs = (
        (sea_hbm, sea_ref),
        (bottom_hbm, bottom_ref),
        (u_hbm, u_ref),
        (v_hbm, v_ref),
        (ix_hbm, ix_ref),
        (fx_hbm, fx_ref),
        (fy_hbm, fy_ref),
        (iy_hbm, iy_ref),
    )
    loads = [pltpu.make_async_copy(src, dst, loaded.at[i]) for i, (src, dst) in enumerate(pairs)]
    for load in loads:
        load.start()
    me_x, me_y = lax.axis_index("gx"), lax.axis_index("gy")
    left, right = (me_x + n - 1) % n, (me_x + 1) % n
    barrier = pltpu.get_barrier_semaphore()
    for d in range(1, n):
        pl.semaphore_signal(barrier, inc=1, device_id={"gx": (me_x + d) % n}, device_id_type=MESH)
    for d in range(1, p):
        pl.semaphore_signal(barrier, inc=1, device_id={"gy": (me_y + d) % p}, device_id_type=MESH)

    table = project_ref[...].astype(F32)
    for level in range(levels):
        for mode in range(2):
            weights[2 * level + mode] = jnp.broadcast_to(
                table[mode : mode + 1, level : level + 1], (ROWS, width)
            )

    def project(ref, out, pad, step):
        at = pl.ds(pl.multiple_of(step * ROWS, ROWS), ROWS)
        depth = depth_of(sea_ref, bottom_ref, at)
        sums = [jnp.zeros((ROWS, width), F32)] * 2
        for level in range(levels):
            value = jnp.where(level < depth, ref[level, at, :].astype(F32), 0.0)
            for mode in range(2):
                sums[mode] = sums[mode] + weights[2 * level + mode] * value
        to = pl.ds(pl.multiple_of(step * ROWS + pad, 8), ROWS)
        for mode in range(2):
            out[mode, to, :] = sums[mode].astype(BF16).astype(F32)

    def edges(first, second, out):
        lane = lax.broadcasted_iota(jnp.int32, (rows, width), 1)
        out[0] = jnp.where(lane == 0, first, pltpu.roll(second, 1, 1)).astype(BF16)
        out[1] = jnp.where(lane == width - 1, first, pltpu.roll(second, width - 1, 1)).astype(BF16)

    def swap_y(src, dst, send, recv, act):
        down = remote(src.at[0], dst.at[1], send.at[0], recv.at[1], gy=jnp.maximum(me_y - 1, 0))
        up = remote(src.at[1], dst.at[0], send.at[1], recv.at[0], gy=jnp.minimum(me_y + 1, p - 1))

        @pl.when(me_y > 0)
        def _():
            if act == "start":
                down.start()
            if act == "send":
                down.wait_send()
            if act == "recv":
                up.wait_recv()

        @pl.when(me_y < p - 1)
        def _():
            if act == "start":
                up.start()
            if act == "send":
                up.wait_send()
            if act == "recv":
                down.wait_recv()

    def difference_y(field, halo, mode):
        lane = lax.broadcasted_iota(jnp.int32, (rows, width), 1)
        low, high = halo[0].astype(F32), halo[1].astype(F32)
        before = jnp.where(lane == 0, pltpu.roll(low, 1 + mode, 1), pltpu.roll(field, 1, 1))
        after = jnp.where(
            lane == width - 1, pltpu.roll(high, width - 1 - mode, 1), pltpu.roll(field, width - 1, 1)
        )
        return 0.5 * (after - before)

    @pl.when(me_y == 0)
    def _():
        yrecv[0] = jnp.zeros((rows, width), BF16)
        precv[0] = jnp.zeros((rows, width), BF16)

    @pl.when(me_y == p - 1)
    def _():
        yrecv[1] = jnp.zeros((rows, width), BF16)
        precv[1] = jnp.zeros((rows, width), BF16)

    steps = rows // ROWS
    for load in loads[:3]:
        load.wait()
    project(u_ref, fu, PAD, 0)
    project(u_ref, fu, PAD, steps - 1)
    xsend[...] = jnp.zeros(xsend.shape, F32)
    for mode in range(2):
        xsend[0, mode : mode + 1, :] = fu[mode, PAD : PAD + 1, :]
        xsend[1, mode : mode + 1, :] = fu[mode, PAD + rows - 1 : PAD + rows, :]

    def project_v(step, carry):
        project(v_ref, fv, 0, step)
        return carry

    loads[3].wait()
    lax.fori_loop(0, steps, project_v, 0)
    edges(fv[0], fv[1], ysend)

    pl.semaphore_wait(barrier, n - 1 + p - 1)
    to_left = remote(xsend.at[0], xrecv.at[1], edge_s.at[0], edge_r.at[0], gx=left)
    to_right = remote(xsend.at[1], xrecv.at[0], edge_s.at[1], edge_r.at[1], gx=right)
    to_left.start()
    to_right.start()

    def project_u(step, carry):
        project(u_ref, fu, PAD, step)
        return carry

    swap_y(ysend, yrecv, ye_s, ye_r, "start")
    lax.fori_loop(1, steps - 1, project_u, 0)

    to_left.wait_recv()
    to_right.wait_recv()
    for mode in range(2):
        fu[mode, PAD - 1 : PAD, :] = xrecv[0, mode : mode + 1, :]
        fu[mode, PAD + rows : PAD + rows + 1, :] = xrecv[1, mode : mode + 1, :]
    swap_y(ysend, yrecv, ye_s, ye_r, "recv")
    sea = sea_ref[...].astype(F32)
    mine = pl.ds(pl.multiple_of(me_x * rows, ROWS), rows)
    modes = range(2)
    gx1 = [AcrossX(n, rows, xg.at[m], as1.at[m], ar1.at[m], ps1.at[m], pr1.at[m]) for m in modes]
    gx2 = [AcrossX(n, rows, xg2.at[m], as2.at[m], ar2.at[m], ps2.at[m], pr2.at[m]) for m in modes]
    gy1 = [AcrossY(p, ysrc.at[m], yg.at[m], ys1.at[m], yr1.at[m]) for m in modes]
    gy2 = [AcrossY(p, ysrc2.at[m], yg2.at[m], ys2.at[m], yr2.at[m]) for m in modes]
    for mode in modes:
        along_x = 0.5 * (
            fu[mode, PAD + 1 : PAD + 1 + rows, :] - fu[mode, PAD - 1 : PAD - 1 + rows, :]
        )
        along_y = difference_y(fv[mode], yrecv, mode)
        xg[mode, mine, :] = (sea * (along_x + along_y)).astype(BF16)
        gx1[mode].start()

    for load in loads[4:]:
        load.wait()
    rows_left = remote(ix_ref.at[0:ROWS], ixe.at[ROWS : 2 * ROWS], edge_s.at[2], edge_r.at[2], gx=left)
    rows_right = remote(
        ix_ref.at[rows - ROWS : rows], ixe.at[0:ROWS], edge_s.at[3], edge_r.at[3], gx=right
    )
    rows_left.start()
    rows_right.start()
    row = lax.broadcasted_iota(jnp.int32, (rows, rows), 0)
    column = lax.broadcasted_iota(jnp.int32, (rows, rows), 1)
    ex = jnp.sum(jnp.where(row == column, ex_ref[...], 0.0), axis=1, keepdims=True)
    for mode in modes:
        denom[mode] = ex + ey_ref[...] + shift_ref[mode]
    for mode in modes:
        gx1[mode].finish()
        ysrc[mode] = jnp.dot(fx_ref[...], xg[mode], preferred_element_type=F32).astype(BF16)
        gy1[mode].start()

    def whole(blocks, mode):
        return jnp.concatenate([blocks[mode, source] for source in range(p)], axis=1)

    for mode in modes:
        gy1[mode].finish()
        spectrum = lax.dot_general(whole(yg, mode), fy_ref[...], LAST, preferred_element_type=F32)
        ysrc2[mode] = (spectrum / denom[mode]).astype(BF16)
        gy2[mode].start()
    for mode in modes:
        gy2[mode].finish()
        back = lax.dot_general(whole(yg2, mode), iy_ref[...], LAST, preferred_element_type=F32)
        xg2[mode, mine, :] = back.astype(BF16)
        gx2[mode].start()
    rows_left.wait_recv()
    rows_right.wait_recv()
    for mode in modes:
        gx2[mode].finish()
        field = jnp.dot(ix_ref[...], xg2[mode], preferred_element_type=F32)
        p_ref[mode] = field
        pp[mode, PAD : PAD + rows, :] = field
    edges(p_ref[0], p_ref[1], psend)
    swap_y(psend, precv, pe_s, pe_r, "start")
    for mode in modes:
        outside = jnp.dot(ixe[...], xg2[mode], preferred_element_type=F32)
        pp[mode, PAD - 1 : PAD, :] = outside[ROWS - 1 : ROWS]
        pp[mode, PAD + rows : PAD + rows + 1, :] = outside[ROWS : ROWS + 1]
        gx_ref[mode] = 0.5 * (
            pp[mode, PAD + 1 : PAD + 1 + rows, :] - pp[mode, PAD - 1 : PAD - 1 + rows, :]
        )
    for copy in gx1 + gx2 + gy1 + gy2 + [to_left, to_right, rows_left, rows_right]:
        copy.wait_send()
    swap_y(ysend, yrecv, ye_s, ye_r, "send")
    swap_y(psend, precv, pe_s, pe_r, "recv")
    for mode in modes:
        gy_ref[mode] = difference_y(p_ref[mode], precv, mode)
    swap_y(psend, precv, pe_s, pe_r, "send")


def body(
    n,
    p,
    u_flow,
    v_flow,
    sea_mask,
    bottom_level,
    mode_project,
    mode_shape,
    forward_x,
    forward_y,
    inverse_x,
    inverse_y,
    eigen_x,
    eigen_y,
    mode_shift,
):
    levels, rows, width = u_flow.shape
    nx, ny = n * rows, p * width
    vmem = pl.BlockSpec(memory_space=pltpu.VMEM)
    smem = pl.BlockSpec(memory_space=pltpu.SMEM)
    dma = pltpu.SemaphoreType.DMA
    chips = n // 2
    field = jax.ShapeDtypeStruct((2, rows, width), F32)
    grad_x, grad_y, pressure = pl.pallas_call(
        functools.partial(kernel, n, p),
        out_shape=(field,) * 3,
        in_specs=[pl.BlockSpec(memory_space=pl.ANY)] * 8 + [vmem] * 3 + [smem],
        out_specs=(vmem,) * 3,
        scratch_shapes=[
            pltpu.VMEM(source.shape, source.dtype)
            for source in (
                u_flow, v_flow, sea_mask, bottom_level, forward_x, forward_y, inverse_x, inverse_y
            )
        ]
        + [dma((8,))]
        + [
            pltpu.VMEM((2 * levels, ROWS, width), F32),
            pltpu.VMEM((2, rows + 2 * PAD, width), F32),
            pltpu.VMEM((2, rows, width), F32),
            pltpu.VMEM((2, 8, width), F32),
            pltpu.VMEM((2, 8, width), F32),
            pltpu.VMEM((2, rows, width), BF16),
            pltpu.VMEM((2, rows, width), BF16),
            pltpu.VMEM((2, nx, width), BF16),
            pltpu.VMEM((2, nx, width), BF16),
            pltpu.VMEM((2, rows, width), BF16),
            pltpu.VMEM((2, rows, width), BF16),
            pltpu.VMEM((2, p, rows, width), BF16),
            pltpu.VMEM((2, p, rows, width), BF16),
            pltpu.VMEM((2 * ROWS, nx), BF16),
            pltpu.VMEM((2, rows + 2 * PAD, width), F32),
            pltpu.VMEM((2, rows, width), BF16),
            pltpu.VMEM((2, rows, width), BF16),
            pltpu.VMEM((2, rows, width), F32),
            dma((4,)),
            dma((4,)),
            dma((2,)),
            dma((2,)),
            dma((2,)),
            dma((2,)),
        ]
        + [dma((2, chips))] * 8
        + [dma((2, p))] * 4,
        compiler_params=pltpu.CompilerParams(
            collective_id=0, has_side_effects=True, vmem_limit_bytes=56 * 2**20
        ),
        cost_estimate=pl.CostEstimate(
            flops=8 * rows * width * (nx + ny), bytes_accessed=8 * u_flow.size, transcendentals=0
        ),
    )(
        u_flow,
        v_flow,
        sea_mask,
        bottom_level,
        forward_x,
        forward_y,
        inverse_x,
        inverse_y,
        mode_project.T,
        eigen_x[None],
        eigen_y[None],
        mode_shift,
    )
    part = rows // 3 if rows % (3 * ROWS) == 0 else rows
    flat = pl.BlockSpec((part, width), lambda i: (i, 0))
    modal = pl.BlockSpec((2, part, width), lambda i: (0, i, 0))
    tall = pl.BlockSpec((levels, part, width), lambda i: (0, i, 0))
    return pl.pallas_call(
        rebuild_kernel,
        out_shape=(
            jax.ShapeDtypeStruct(u_flow.shape, BF16),
            jax.ShapeDtypeStruct(v_flow.shape, BF16),
            field,
        ),
        grid=(rows // part,),
        in_specs=[modal] * 3 + [flat] * 2 + [smem],
        out_specs=(tall, tall, modal),
        compiler_params=pltpu.CompilerParams(vmem_limit_bytes=56 * 2**20),
        cost_estimate=pl.CostEstimate(
            flops=8 * u_flow.size, bytes_accessed=4 * u_flow.size, transcendentals=0
        ),
    )(grad_x, grad_y, pressure, sea_mask, bottom_level, mode_shape.T)


def solution(mesh):
    return jax.shard_map(
        functools.partial(body, mesh.shape["gx"], mesh.shape["gy"]),
        mesh=mesh,
        in_specs=(
            P(None, "gx", "gy"),
            P(None, "gx", "gy"),
            P("gx", "gy"),
            P("gx", "gy"),
            P(),
            P(),
            P("gx", None),
            P("gy", None),
            P("gx", None),
            P("gy", None),
            P("gx"),
            P("gy"),
            P(),
        ),
        out_specs=(P(None, "gx", "gy"), P(None, "gx", "gy"), P(None, "gx", "gy")),
        check_vma=False,
    )
```
